512 devices in a mesh: rep: 16 (over y, x_hi, core), fsdp: 32 (over x_lo, z).
Axes of the slice: x: 4 (x_hi: 2, x_lo: 2; x = x_hi * 2 + x_lo), y: 4, z: 16, core: 2. Of those that a mesh axis runs over, the one named last changes fastest.
Arguments:
- codes: int32 [16, 4194304], P('rep', 'fsdp'), may hold values from 0 to 15
- scales: float32 [16, 65536], P('rep', 'fsdp'), may hold values from 0.02 to 0.3
- base: float32 [4194304], P('fsdp'), may hold values from -6 to 6
- momentum: float32 [4194304], P('fsdp'), may hold values from -3 to 3
- inputs: bfloat16 [16, 4096, 8192], P('rep', 'fsdp'), may hold values from -30 to 30
- gain: bfloat16 [16, 8192], P('rep', 'fsdp'), may hold values from 0.099609375 to 1.8984375
- cotangent: bfloat16 [16, 4096, 512], P('rep', 'fsdp'), may hold values from -0.25 to 0.25
Outputs:
- new_base: float32 [4194304], P('fsdp')
- new_momentum: float32 [4194304], P('fsdp')
- keys: bfloat16 [16, 4096, 512], P('rep', 'fsdp')
- grad_weight: float32 [16, 8192, 512], P('rep', 'fsdp')
- grad_gain: float32 [16, 8192], P('rep', 'fsdp')
The draws below stay inside these ranges and needn't reach their ends.
Inputs may be any that keep to these rules, and one draw needn't show every extreme that they name: `codes`: each entry is one 4-bit code.
All inputs are finite; a program needn't handle non-finite values.
Results may differ from the reference program's by a relative error of at most 0.015.
Values may be sent and summed in bfloat16 or wider, within the bound.
A program may use at most 64 MiB of HBM per device.

```python
import math
import jax
import jax.numpy as jnp
from jax import lax

D = 8192
KV = 512
TOKENS_REP = 4096
F = 4194304
BLOCK = 64
N_REP = 16
N_FSDP = 32


def draw_inputs(key, part):
    key = jax.random.fold_in(key, 11)
    first, second, third = jax.random.split(key, 3)
    shape = (N_REP, TOKENS_REP, D)
    row_scale = jnp.exp(jax.random.uniform(first, (N_REP, TOKENS_REP, 1), jnp.float32, math.log(0.3), math.log(3.0)))
    col_scale = jnp.exp(jax.random.uniform(second, (1, 1, D), jnp.float32, math.log(0.3), math.log(3.0)))
    values = jax.random.normal(third, shape, jnp.float32)
    return jnp.clip(values * row_scale * col_scale, -30.0, 30.0).astype(jnp.bfloat16)


def touch_ends(drawn, stream_key, least, top_value):
    extent = drawn.shape
    index_at = [jax.random.randint(jax.random.fold_in(stream_key, axis), (), 0, extent[axis]) for axis in range(len(extent))]
    drawn = drawn.at[tuple(index_at)].set(least)
    longest = extent.index(max(extent))
    index_at[longest] = (index_at[longest] + 1) % extent[longest]
    return drawn.at[tuple(index_at)].set(top_value)


def levels(stream_key, dims, pieces, least, top_value):
    def one(position, blocks):
        draws = jax.random.uniform(jax.random.fold_in(jax.random.fold_in(stream_key, 6), position), (blocks,), jnp.float32, least / len(pieces), top_value / len(pieces))
        return jnp.repeat(jnp.exp(draws), dims[position] // blocks).reshape((-1,) + (1,) * (len(dims) - position - 1))

    loudness = one(*pieces[0])
    for cut in pieces[1:]:
        loudness = loudness * one(*cut)
    return loudness


def scatter_about(rng, dims, deviation, most, cuts=(), held_as=jnp.bfloat16):
    loudness = levels(rng, dims, cuts, -0.22, 0.18) if cuts else 1.0
    drawn = jax.random.normal(rng, dims, jnp.float32) * deviation * loudness
    return jnp.minimum(jnp.maximum(drawn, -most), most).astype(held_as)


def setup_inputs(seed: int = 0) -> dict:
    key_of = jax.random.split(jax.random.key(seed), 8)
    codes = touch_ends(jax.random.randint(key_of[0], (N_REP, F), 0, 16), jax.random.fold_in(key_of[0], 1), 0, 15).astype(jnp.int32)
    scales = jnp.clip(jnp.exp(math.log(0.3) - 2.7080503 * jax.random.uniform(key_of[1], (N_REP, F // BLOCK), jnp.float32) ** levels(key_of[1], (N_REP, F // BLOCK), ((0, 16), (1, 32)), -0.2, 0.2)), 0.02, 0.3)
    base = scatter_about(key_of[2], (F,), 1.0, 6.0, ((0, 32),), jnp.float32)
    momentum = scatter_about(key_of[3], (F,), 0.5, 3.0, ((0, 32),), jnp.float32)
    inputs = draw_inputs(jax.random.fold_in(key_of[7], 71), 0)
    gain = jnp.clip(1.0 + 0.18 * jax.random.normal(key_of[5], (N_REP, D), jnp.float32), 0.099609375, 1.8984375).astype(jnp.bfloat16)
    cotangent = scatter_about(key_of[6], (N_REP, TOKENS_REP, KV), (TOKENS_REP ** -0.5), 0.25, ((0, 16), (1, 32)))
    return {"codes": codes, "scales": scales, "base": base, "momentum": momentum, "inputs": inputs, "gain": gain, "cotangent": cotangent}


outer_rate = 0.7
momentum_decay = 0.9

def reference(codes, scales, base, momentum, inputs, gain, cotangent):
    decoded = (codes - 8).astype(jnp.float32) * jnp.repeat(scales, BLOCK, axis=1)
    average = lax.optimization_barrier(jnp.sum(decoded, axis=0)) / N_REP
    new_momentum = momentum_decay * momentum + average
    new_base = base - outer_rate * (average + momentum_decay * new_momentum)
    projection = (new_base.reshape(D, KV) * D ** (-0.5)).astype(jnp.bfloat16)
    group_rows = D // N_FSDP

    def one_replica(items):
        values, gains, upstream = items
        wide = values.astype(jnp.float32)
        inv_rms = lax.rsqrt(lax.optimization_barrier(jnp.mean(wide * wide, axis=1, keepdims=True)) + 1e-05)
        normed = (wide * inv_rms * gains.astype(jnp.float32)).astype(jnp.bfloat16)

        def add_group(total, group):
            start = group * group_rows
            cols = lax.dynamic_slice_in_dim(normed, start, group_rows, 1)
            rows = lax.dynamic_slice_in_dim(projection, start, group_rows, 0)
            part = jnp.dot(cols, rows, preferred_element_type=jnp.float32)
            part = lax.optimization_barrier(part.astype(jnp.bfloat16)).astype(jnp.float32)
            return (total + part, None)
        start_total = jnp.zeros((TOKENS_REP, KV), jnp.float32)
        key_total, unused = lax.scan(add_group, start_total, jnp.arange(N_FSDP, dtype=jnp.int32))
        grad_w = jnp.dot(normed.T, upstream, preferred_element_type=jnp.float32)
        back = jnp.dot(upstream, projection.T, preferred_element_type=jnp.float32)
        grad_g = lax.optimization_barrier(jnp.sum(back * wide * inv_rms, axis=0))
        return (key_total.astype(jnp.bfloat16), grad_w, grad_g)
    keys, grad_weight, grad_gain = lax.map(one_replica, (inputs, gain, cotangent))
    return (new_base, new_momentum, keys, grad_weight, grad_gain)
```

```python
import functools

import jax
import jax.numpy as jnp
from jax import lax
from jax.experimental import pallas as pl
from jax.experimental.pallas import tpu as pltpu
from jax.sharding import PartitionSpec as P

MESH = pl.DeviceIdType.MESH
F32 = jnp.float32
BF16 = jnp.bfloat16

D = 8192
KV = 512
REP = 16
Z = 16
OWN = 256
TOK = 128
SUBS = 2
PART = OWN // SUBS
STEPS = 8
outer_rate = 0.7
momentum_decay = 0.9


def whole_wait(ref, sem):
    pltpu.make_async_copy(ref, ref, sem).wait()


def kernel(
    codes, scales, base, momentum, inputs, gain, cotangent,
    new_base, new_momentum, keys, grad_weight, grad_gain,
    decoded, pieces, averages, rows, weight, gains, halves, both, inverse,
    totals, landed, terms, key_total,
    piece_send, piece_recv, average_send, average_recv,
    half_send, half_recv, up_send, up_recv, gain_send, gain_recv,
    gain_z_send, gain_z_recv,
    sum_send, sum_recv, wz_send, wz_recv, wx_send, wx_recv, wy_send, wy1_recv, wy2_recv, wc_send, wc_recv,
):
    rep = lax.axis_index("rep")
    shard = lax.axis_index("fsdp")
    core = rep % 2
    x_hi = (rep // 2) % 2
    y = rep // 4
    x_lo = shard // Z
    z = shard % Z
    x = x_hi * 2 + x_lo

    def at(y_to=y, x_to=x, z_to=z, core_to=core):
        return ((y_to * 2 + x_to // 2) * 2 + core_to, (x_to % 2) * Z + z_to)

    up_z, down_z = at(z_to=(z + 1) % Z), at(z_to=(z + Z - 1) % Z)
    ring = (up_z, down_z)
    right, left = at(x_to=(x + 1) % 4), at(x_to=(x + 3) % 4)
    across = at(x_to=(x + 2) % 4)
    north, south = at(y_to=(y + 1) % 4), at(y_to=(y + 3) % 4)
    twin = at(core_to=1 - core)
    partner = at(x_to=x_hi * 2 + 1 - x_lo)

    def send(src, dst, send_sem, recv_sem, device):
        copy = pltpu.make_async_remote_copy(
            src_ref=src, dst_ref=dst, send_sem=send_sem, recv_sem=recv_sem,
            device_id=device, device_id_type=MESH,
        )
        copy.start()

    barrier = pltpu.get_barrier_semaphore()

    def greet(step, carry):
        pl.semaphore_signal(barrier, inc=1, device_id=((rep + step) % REP, shard), device_id_type=MESH)
        return carry

    lax.fori_loop(1, REP, greet, 0)
    for device in (up_z, down_z, right, left):
        pl.semaphore_signal(barrier, inc=1, device_id=device, device_id_type=MESH)

    entry = lax.broadcasted_iota(jnp.int32, (64, 128), 0)
    lane = lax.broadcasted_iota(jnp.int32, (64, 128), 1)
    chosen = (lane >> 1) == entry
    from_lane = lax.broadcasted_iota(jnp.int32, (128, 128), 0)
    to_lane = lax.broadcasted_iota(jnp.int32, (128, 128), 1)
    spread = ((from_lane & 1) == (to_lane >> 6)).astype(BF16)

    def decode(block, carry):
        picked = jnp.where(chosen, scales[pl.ds(block, 1), :], 0.0)
        high = picked.astype(BF16)
        low = (picked - high.astype(F32)).astype(BF16)
        scale = jnp.dot(high, spread, preferred_element_type=F32) + jnp.dot(low, spread, preferred_element_type=F32)
        code = codes[pl.ds(pl.multiple_of(block * 64, 64), 64), :]
        decoded[block] = ((code - 8).astype(F32) * scale).astype(BF16)
        return carry

    lax.fori_loop(0, REP, decode, 0)

    def squares(block, total):
        cols = inputs[:, pl.ds(pl.multiple_of(block * 512, 512), 512)].astype(F32)
        cols = cols * cols
        return total + (cols[:, :128] + cols[:, 128:256]) + (cols[:, 256:384] + cols[:, 384:])

    square = lax.fori_loop(0, D // 512, squares, jnp.zeros((TOK, 128), F32))
    inv = lax.rsqrt(jnp.sum(square, axis=1, keepdims=True) * (1.0 / D) + 1e-05)
    inverse[...] = jnp.broadcast_to(inv, (TOK, 128))
    both[0] = (cotangent[...].astype(F32) * inv).astype(BF16)
    own_gain = gain[...].astype(F32)
    gains[pl.ds(z * 2 + x_lo, 1)] = own_gain.reshape(1, 1, OWN)

    pl.semaphore_wait(barrier, REP - 1 + 4)

    def send_piece(step, carry):
        peer = (rep + step) % REP
        send(decoded.at[peer], pieces.at[step - 1], piece_send, piece_recv, (peer, shard))
        return carry

    lax.fori_loop(1, REP, send_piece, 0)

    def send_half(far):
        target = (z + far) % Z
        start = pl.multiple_of(((1 - x_lo) * Z + target) * OWN, OWN)
        send(inputs.at[:, pl.ds(start, OWN)], halves.at[target], half_send, half_recv.at[far], partner)

    order = [8]
    for far in range(7, 0, -1):
        order += [far, Z - far]
    order += [0]
    sent_halves = [0]

    def more_halves(count):
        for far in order[sent_halves[0]: sent_halves[0] + count]:
            send_half(far)
        sent_halves[0] += count

    send(both.at[0], both.at[1], up_send, up_recv, partner)
    more_halves(1)
    send(gains.at[z * 2 + x_lo], gains.at[z * 2 + x_lo], gain_send, gain_recv, partner)
    more_halves(2)

    def term(far, slot):
        target = (z + far) % Z
        whole_wait(halves.at[target], half_recv.at[far])
        start = pl.multiple_of((x_lo * Z + target) * OWN, OWN)
        cols = jnp.concatenate([inputs[:, pl.ds(start, OWN)], halves[target]], axis=0)
        terms[slot] = lax.dot_general(
            cols, both[...].reshape(2 * TOK, KV), (((0,), (0,)), ((), ())), preferred_element_type=F32
        )

    def send_sum(step, way, sub):
        part = pl.ds(sub * PART, PART)
        send(
            totals.at[way, step - 1, part], landed.at[way, step - 1, part],
            sum_send.at[way, min(step - 1, 1)], sum_recv.at[way, step - 1, sub], ring[way],
        )

    def first_way(sub):
        return 0 if sub < SUBS // 2 else 1

    def sum_unit(step, way, sub):
        part = pl.ds(sub * PART, PART)
        value = terms[way, part]
        if step > 2 or first_way(sub) == way:
            whole_wait(landed.at[way, step - 2, part], sum_recv.at[way, step - 2, sub])
            value = value + landed[way, step - 2, part].astype(F32)
        totals[way, step - 1, part] = value.astype(BF16)
        send_sum(step, way, sub)

    whole_wait(both.at[1], up_recv)
    term(8, 0)
    for sub in range(SUBS):
        way = first_way(sub)
        part = pl.ds(sub * PART, PART)
        totals[way, 0, part] = terms[0, part].astype(BF16)
        send_sum(1, way, sub)
    more_halves(2)

    whole_wait(pieces, piece_recv)

    def add_piece(step, total):
        return total + pieces[step].astype(F32)

    total = lax.fori_loop(0, REP - 1, add_piece, decoded[rep].astype(F32))
    average = (total * (1.0 / REP)).astype(BF16)
    averages[rep] = average
    average = average.astype(F32)

    def send_average(step, carry):
        send(averages.at[rep], averages.at[rep], average_send, average_recv, ((rep + step) % REP, shard))
        return carry

    own = pl.ds(pl.multiple_of(rep * 64, 64), 64)
    moved = momentum_decay * momentum[own, :] + average
    rows[...] = (base[own, :] - outer_rate * (average + momentum_decay * moved)) * D ** (-0.5)

    def block_at(z_at, core_at=core, y_at=y, x_at=x):
        return ((z_at * 2 + core_at) * 4 + y_at) * 4 + x_at

    mine = block_at(z)
    for col in range(4):
        weight[pl.ds(mine, 1), :, col * 128:(col + 1) * 128] = (
            rows[pl.ds(col, 16, stride=4), :].astype(BF16).reshape(1, 16, 128)
        )

    def send_weight_z(step):
        for way in range(2 if step < STEPS else 1):
            source = (z + Z - (step - 1)) % Z if way == 0 else (z + step - 1) % Z
            block = weight.at[block_at(source)]
            send(block, block, wz_send.at[way], wz_recv.at[way, step - 1], ring[way])
            block = gains.at[pl.ds(source * 2, 2)]
            send(block, block, gain_z_send.at[way], gain_z_recv.at[way, step - 1], ring[way])

    whole_wait(gains.at[0], gain_recv)
    send_weight_z(1)
    lax.fori_loop(1, REP, send_average, 0)

    def slices(group):
        if group in (0, STEPS):
            return ((z + group) % Z,)
        return ((z + Z - group) % Z, (z + group) % Z)

    def arrived_z(group):
        for way in range(2 if group < STEPS else 1):
            whole_wait(weight.at[0], wz_recv.at[way, group - 1])
            whole_wait(gains.at[pl.ds(0, 2)], gain_z_recv.at[way, group - 1])

    def send_x(group):
        for at_z in slices(group):
            block = weight.at[block_at(at_z)]
            for device in (right, left, across):
                send(block, block, wx_send, wx_recv.at[group], device)

    def send_y1(group):
        held = slices(group)
        whole_wait(weight.at[pl.ds(0, 3 * len(held))], wx_recv.at[group])
        for at_z in held:
            block = weight.at[pl.ds(block_at(at_z, x_at=0), 4)]
            for device in (north, south):
                send(block, block, wy_send, wy1_recv.at[group], device)

    def send_y2(group):
        held = slices(group)
        whole_wait(weight.at[pl.ds(0, 8 * len(held))], wy1_recv.at[group])
        for way, at_z in enumerate(held):
            y_from = (y + 3) % 4 if way == 0 else (y + 1) % 4
            block = weight.at[pl.ds(block_at(at_z, y_at=y_from, x_at=0), 4)]
            send(block, block, wy_send, wy2_recv.at[group], (north, south)[way])

    def send_core(group):
        held = slices(group)
        whole_wait(weight.at[pl.ds(0, 4 * len(held))], wy2_recv.at[group])
        for at_z in held:
            block = weight.at[pl.ds(block_at(at_z, y_at=0, x_at=0), 16)]
            send(block, block, wc_send, wc_recv.at[group], twin)

    def project(group):
        held = slices(group)
        whole_wait(weight.at[pl.ds(0, 16 * len(held))], wc_recv.at[group])
        for at_z in held:
            def one(lo, carry):
                start = pl.multiple_of((lo * Z + at_z) * OWN, OWN)
                scale = jnp.concatenate([inverse[...]] * 2, axis=1)
                normed = inputs[:, pl.ds(start, OWN)].astype(F32) * scale * gains[at_z * 2 + lo]
                parts = [
                    weight[block_at(at_z, member % 2, member // 4, ((member // 2) % 2) * 2 + lo)]
                    for member in range(REP)
                ]
                value = jnp.dot(
                    normed.astype(BF16), jnp.concatenate(parts, axis=0), preferred_element_type=F32
                )
                key_total[...] += value.astype(BF16).astype(F32)
                return carry

            lax.fori_loop(0, 2, one, 0)

    def outer_step():
        whole_wait(averages.at[pl.ds(0, REP - 1)], average_recv)

        def one(block, carry):
            at_rows = pl.ds(pl.multiple_of(block * 64, 64), 64)
            average = averages[block].astype(F32)
            moved = momentum_decay * momentum[at_rows, :] + average
            new_momentum[at_rows, :] = moved
            new_base[at_rows, :] = base[at_rows, :] - outer_rate * (average + momentum_decay * moved)
            return carry

        lax.fori_loop(0, REP, one, 0)

    key_total[...] = jnp.zeros_like(key_total)
    send_x(0)

    stages = (send_y1, send_y2, send_core, project)

    def weight_slot(slot):
        if 1 <= slot <= STEPS:
            arrived_z(slot)
            if slot < STEPS:
                send_weight_z(slot + 1)
            send_x(slot)
        for behind, stage in enumerate(stages):
            group = slot - 1 - behind
            if 0 <= group <= STEPS:
                stage(group)

    slot = 1
    for step in range(2, STEPS + 1):
        term(9 - step, 0)
        term(Z - (9 - step), 1)
        more_halves(3)
        for sub in range(SUBS):
            for way in range(2):
                sum_unit(step, way, sub)
            weight_slot(slot)
            slot += 1
            if slot == 4:
                outer_step()
    while slot - 1 - len(stages) < STEPS:
        weight_slot(slot)
        slot += 1
    keys[...] = key_total[...].astype(BF16)

    term(0, 0)
    gain_col = jnp.transpose(jnp.broadcast_to(own_gain, (128, OWN)))
    dots = jnp.zeros((OWN, 128), F32)
    for sub in range(SUBS):
        for way in range(2):
            part = pl.ds(sub * PART, PART)
            whole_wait(landed.at[way, STEPS - 1, part], sum_recv.at[way, STEPS - 1, sub])
    for col in range(4):
        cols = slice(col * 128, (col + 1) * 128)
        value = (
            terms[0, :, cols] + landed[0, STEPS - 1, :, cols].astype(F32) + landed[1, STEPS - 1, :, cols].astype(F32)
        )
        grad_weight[:, cols] = value * gain_col
        row = (new_base[pl.ds(col, OWN, stride=4), :] * D ** (-0.5)).astype(BF16).astype(F32)
        dots = dots + row * value
    grad_gain[...] = jnp.sum(jnp.transpose(dots), axis=0, keepdims=True)

    whole_wait(pieces, piece_send)
    whole_wait(averages.at[pl.ds(0, REP - 1)], average_send)
    whole_wait(halves, half_send)
    whole_wait(both.at[1], up_send)
    whole_wait(gains.at[0], gain_send)
    for way in range(2):
        whole_wait(totals.at[way, 0, pl.ds(0, OWN // 2)], sum_send.at[way, 0])
        whole_wait(totals.at[way, pl.ds(1, STEPS - 1)], sum_send.at[way, 1])
        count = STEPS - way
        whole_wait(weight.at[pl.ds(0, count)], wz_send.at[way])
        whole_wait(gains.at[pl.ds(0, 2 * count)], gain_z_send.at[way])
    whole_wait(weight.at[pl.ds(0, 3 * Z)], wx_send)
    whole_wait(weight.at[pl.ds(0, 12 * Z)], wy_send)
    whole_wait(weight.at[pl.ds(0, 16 * Z)], wc_send)


def shards(codes, scales, base, momentum, inputs, gain, cotangent):
    vmem = pl.BlockSpec(memory_space=pltpu.VMEM)
    dma = pltpu.SemaphoreType.DMA
    out = pl.pallas_call(
        kernel,
        out_shape=(
            jax.ShapeDtypeStruct((1024, 128), F32),
            jax.ShapeDtypeStruct((1024, 128), F32),
            jax.ShapeDtypeStruct((TOK, KV), BF16),
            jax.ShapeDtypeStruct((OWN, KV), F32),
            jax.ShapeDtypeStruct((1, OWN), F32),
        ),
        in_specs=[vmem] * 7,
        out_specs=[vmem] * 5,
        scratch_shapes=[
            pltpu.VMEM((REP, 64, 128), BF16),
            pltpu.VMEM((REP - 1, 64, 128), BF16),
            pltpu.VMEM((REP, 64, 128), BF16),
            pltpu.VMEM((64, 128), F32),
            pltpu.VMEM((512, 16, KV), BF16),
            pltpu.VMEM((2 * Z, 1, OWN), F32),
            pltpu.VMEM((Z, TOK, OWN), BF16),
            pltpu.VMEM((2, TOK, KV), BF16),
            pltpu.VMEM((TOK, 128), F32),
            pltpu.VMEM((2, STEPS, OWN, KV), BF16),
            pltpu.VMEM((2, STEPS, OWN, KV), BF16),
            pltpu.VMEM((2, OWN, KV), F32),
            pltpu.VMEM((TOK, KV), F32),
            dma, dma, dma, dma,
            dma, dma((Z,)), dma, dma, dma, dma,
            dma((2,)), dma((2, STEPS)),
            dma((2, 2)), dma((2, STEPS, SUBS)), dma((2,)), dma((2, STEPS)),
            dma, dma((STEPS + 1,)), dma, dma((STEPS + 1,)), dma((STEPS + 1,)), dma, dma((STEPS + 1,)),
        ],
        compiler_params=pltpu.CompilerParams(
            collective_id=0, has_side_effects=True, vmem_limit_bytes=56 * 1024 * 1024
        ),
    )(
        codes.reshape(1024, 128), scales.reshape(16, 128), base.reshape(1024, 128), momentum.reshape(1024, 128),
        inputs[0], gain, cotangent[0],
    )
    new_base, new_momentum, keys, grad_weight, grad_gain = out
    return new_base.reshape(-1), new_momentum.reshape(-1), keys[None], grad_weight[None], grad_gain


def solution(mesh):
    placed = (
        P("rep", "fsdp"),
        P("rep", "fsdp"),
        P("fsdp"),
        P("fsdp"),
        P("rep", "fsdp", None),
        P("rep", "fsdp"),
        P("rep", "fsdp", None),
    )
    return jax.shard_map(
        shards,
        mesh=mesh,
        in_specs=placed,
        out_specs=(
            P("fsdp"),
            P("fsdp"),
            P("rep", "fsdp", None),
            P("rep", "fsdp", None),
            P("rep", "fsdp"),
        ),
        check_vma=False,
    )
```

```python
import jax
import jax.numpy as jnp
from jax import lax
from jax.experimental import pallas as pl
from jax.experimental.pallas import tpu as pltpu
from jax.sharding import PartitionSpec as P

MESH = pl.DeviceIdType.MESH
F32 = jnp.float32
BF16 = jnp.bfloat16

D = 8192
KV = 512
Z = 16
OWN = 256
TOK = 128
SUBS = 4
PART = KV // SUBS
STEPS = 8
outer_rate = 0.7
momentum_decay = 0.9

HOPS = (
    ((0, 5), (0, 11)),
    ((0, 1), (0, 15), (5, 1), (5, 15), (-5, 1), (-5, 15), (-5, 3)),
    ((-1, 1), (4, 1), (-6, 1), (1, 15), (-4, 15), (6, 15)),
)
GROUPS = ((0,), (5, -5), (1, -1, 4, -4, 6, -6, 8), (2, -2, 3, -3, 7, -7))
Y_FIRST = (6, -6, 8, 7, -7, 3)


def whole_wait(ref, sem):
    pltpu.make_async_copy(ref, ref, sem).wait()


def kernel(
    codes_hbm, scales_hbm, base_hbm, momentum_hbm, inputs_hbm, gain, cotangent_hbm,
    base_out, momentum_out, keys_out, weight_out, gain_out,
    codes, scales, base, momentum, inputs, cotangent, new_base, new_momentum, keys, grad_weight,
    decoded, twin_part, pairs, pieces, averages, rows, weight, gains, halves, both, inverse,
    normed, twin_normed, totals, landed, terms, key_total, key_twin,
    local_sem, out_sem, twin_send, twin_recv, piece_send, piece_recv,
    average_send, average_recv, average_twin_send, average_twin_recv,
    half_send, half_recv, up_send, up_recv, gain_send, gain_recv, gain_z_send, gain_z_recv,
    normed_send, normed_recv, key_send, key_recv, sum_send, sum_recv, wz_send, wz_recv,
    first_send, first_recv, second_send, second_recv, third_recv,
):
    rep = lax.axis_index("rep")
    shard = lax.axis_index("fsdp")
    core = rep % 2
    x_hi = (rep // 2) % 2
    y = rep // 4
    x_lo = shard // Z
    z = shard % Z
    x = x_hi * 2 + x_lo
    chip = rep // 2
    own = core * 8 + chip

    def at(y_to=y, x_to=x, z_to=z, core_to=core):
        return ((y_to * 2 + x_to // 2) * 2 + core_to, (x_to % 2) * Z + z_to)

    def along_z(by):
        return at(z_to=(z + by) % Z)

    def fellow(step):
        return ((chip + step) % 8) * 2 + core, shard

    ring = (along_z(1), along_z(15))
    right, left, across = (at(x_to=(x + by) % 4) for by in (1, 3, 2))
    north, south, over = (at(y_to=(y + by) % 4) for by in (1, 3, 2))
    twin = at(core_to=1 - core)
    partner = at(x_to=x_hi * 2 + 1 - x_lo)

    def send(src, dst, send_sem, recv_sem, device):
        pltpu.make_async_remote_copy(
            src_ref=src, dst_ref=dst, send_sem=send_sem, recv_sem=recv_sem,
            device_id=device, device_id_type=MESH,
        ).start()

    barrier = pltpu.get_barrier_semaphore()

    def greet(step, carry):
        pl.semaphore_signal(barrier, inc=1, device_id=fellow(step), device_id_type=MESH)
        return carry

    lax.fori_loop(1, 8, greet, 0)
    near = [twin, right, left] + [along_z(by) for by in (1, 15, 5, 11, 3, 13)]
    for device in near:
        pl.semaphore_signal(barrier, inc=1, device_id=device, device_id_type=MESH)

    def load(src, dst, index):
        pltpu.make_async_copy(src, dst, local_sem.at[index]).start()

    load(codes_hbm, codes, 5)
    load(scales_hbm, scales, 6)
    quarter = D // 4
    for index in range(4):
        cols = pl.ds(index * quarter, quarter)
        load(inputs_hbm.at[:, cols], inputs.at[:, cols], index)
    load(cotangent_hbm, cotangent, 4)
    load(base_hbm, base, 7)
    load(momentum_hbm, momentum, 8)

    entry = lax.broadcasted_iota(jnp.int32, (64, 128), 0)
    lane = lax.broadcasted_iota(jnp.int32, (64, 128), 1)
    chosen = (lane >> 1) == entry
    from_lane = lax.broadcasted_iota(jnp.int32, (128, 128), 0)
    to_lane = lax.broadcasted_iota(jnp.int32, (128, 128), 1)
    spread = ((from_lane & 1) == (to_lane >> 6)).astype(BF16)

    def decode(block, carry):
        picked = jnp.where(chosen, scales[pl.ds(block, 1), :], 0.0)
        high = picked.astype(BF16)
        low = (picked - high.astype(F32)).astype(BF16)
        scale = jnp.dot(high, spread, preferred_element_type=F32) + jnp.dot(low, spread, preferred_element_type=F32)
        code = codes[pl.ds(pl.multiple_of(block * 64, 64), 64), :]
        decoded[block] = ((code - 8).astype(F32) * scale).astype(BF16)
        return carry

    whole_wait(codes, local_sem.at[5])
    whole_wait(scales, local_sem.at[6])
    lax.fori_loop(0, 16, decode, 0)

    def squares(block, total):
        cols = inputs[:, pl.ds(pl.multiple_of(block * 512, 512), 512)].astype(F32)
        cols = cols * cols
        return total + (cols[:, :128] + cols[:, 128:256]) + (cols[:, 256:384] + cols[:, 384:])

    square = jnp.zeros((TOK, 128), F32)
    for index in range(4):
        cols = inputs.at[:, pl.ds(index * quarter, quarter)]
        whole_wait(cols, local_sem.at[index])
        square = lax.fori_loop(index * 4, index * 4 + 4, squares, square)
    inv = lax.rsqrt(jnp.sum(square, axis=1, keepdims=True) * (1.0 / D) + 1e-05)
    inverse[...] = jnp.broadcast_to(inv, (TOK, 128))
    whole_wait(cotangent, local_sem.at[4])
    for sub in range(SUBS):
        both[sub, 0] = (cotangent[:, sub * PART:(sub + 1) * PART].astype(F32) * inv).astype(BF16)
    own_gain = gain[...].astype(F32)
    gains[pl.ds(z * 2 + x_lo, 1)] = own_gain.reshape(1, 1, OWN)

    pl.semaphore_wait(barrier, 7 + len(near))

    def send_half(far):
        target = (z + far) % Z
        start = pl.multiple_of(((1 - x_lo) * Z + target) * OWN, OWN)
        send(inputs.at[:, pl.ds(start, OWN)], halves.at[target], half_send, half_recv.at[far], partner)

    def send_up(sub):
        send(both.at[sub, 0], both.at[sub, 1], up_send, up_recv.at[sub], partner)

    send(decoded.at[pl.ds((1 - core) * 8, 8)], twin_part, twin_send, twin_recv, twin)
    send(gains.at[z * 2 + x_lo], gains.at[z * 2 + x_lo], gain_send, gain_recv, partner)
    send_up(0)
    send_half(8)
    for sub in (2, 1, 3):
        send_up(sub)
    send_half(7)
    send_half(9)

    whole_wait(twin_part, twin_recv)
    for block in range(8):
        pairs[block] = (decoded[core * 8 + block].astype(F32) + twin_part[block].astype(F32)).astype(BF16)

    def send_piece(step, carry):
        send(pairs.at[(chip + step) % 8], pieces.at[step - 1], piece_send, piece_recv, fellow(step))
        return carry

    lax.fori_loop(1, 8, send_piece, 0)

    def features(far):
        target = (z + far) % Z
        whole_wait(halves.at[target], half_recv.at[far])
        start = pl.multiple_of((x_lo * Z + target) * OWN, OWN)
        return jnp.concatenate([inputs[:, pl.ds(start, OWN)], halves[target]], axis=0)

    def product(cols, cotangents):
        return lax.dot_general(cols, cotangents, (((0,), (0,)), ((), ())), preferred_element_type=F32)

    def term(far, slot):
        cotangents = jnp.concatenate([both[sub].reshape(2 * TOK, PART) for sub in range(SUBS)], axis=1)
        terms[slot] = product(features(far), cotangents)

    def send_sum(step, way, sub, value):
        totals[way, step - 1, sub] = value.astype(BF16)
        send(
            totals.at[way, step - 1, sub], landed.at[way, step - 1, sub],
            sum_send.at[way, min(step - 1, 1)], sum_recv.at[way, step - 1, sub], ring[way],
        )

    def sum_unit(step, way, sub, fresh=False):
        value = terms[way, :, sub * PART:(sub + 1) * PART]
        if not fresh:
            whole_wait(landed.at[way, step - 2, sub], sum_recv.at[way, step - 2, sub])
            value = value + landed[way, step - 2, sub].astype(F32)
        send_sum(step, way, sub, value)

    cols = features(8)
    for sub in (0, 2, 1, 3):
        whole_wait(both.at[sub, 1], up_recv.at[sub])
        send_sum(1, sub // 2, sub, product(cols, both[sub].reshape(2 * TOK, PART)))
    send_half(6)
    send_half(10)

    def gain_event(level):
        if level == 0:
            whole_wait(gains.at[0], gain_recv)
        else:
            whole_wait(gains.at[pl.ds(0, 2 * len(GROUPS[level]))], gain_z_recv.at[level - 1])
        if level < 3:
            for far, by in HOPS[level]:
                block = gains.at[pl.ds(((z + far + Z) % Z) * 2, 2)]
                send(block, block, gain_z_send, gain_z_recv.at[level], along_z(by))

    gain_event(0)
    term(7, 0)
    term(9, 1)
    for sub in (2, 0, 3, 1):
        sum_unit(2, 1 - sub // 2, sub, fresh=True)
    send_half(5)
    send_half(11)
    for sub in (0, 2, 1, 3):
        sum_unit(2, sub // 2, sub)

    mine = pl.ds(pl.multiple_of(own * 64, 64), 64)

    def slice_at(far):
        return (z + far + Z) % Z

    def start_weight():
        whole_wait(pieces, piece_recv)
        total = pairs[chip].astype(F32)
        for step in range(7):
            total = total + pieces[step].astype(F32)
        average = (total * (1.0 / 16)).astype(BF16)
        averages[own] = average
        average = average.astype(F32)
        whole_wait(base, local_sem.at[7])
        whole_wait(momentum, local_sem.at[8])
        moved = momentum_decay * momentum[mine, :] + average
        rows[...] = (base[mine, :] - outer_rate * (average + momentum_decay * moved)) * D ** (-0.5)
        for col in range(4):
            weight[z, y, x, :, col * 128:(col + 1) * 128] = rows[pl.ds(col, 16, stride=4), :].astype(BF16)
        send_z(0)
        send_first(0)

    def send_averages():
        def one(step, carry):
            send(averages.at[own], averages.at[own], average_send, average_recv, fellow(step))
            return carry

        lax.fori_loop(1, 8, one, 0)

    def swap_averages():
        whole_wait(averages.at[pl.ds(0, 7)], average_recv)
        block = averages.at[pl.ds(core * 8, 8)]
        send(block, block, average_twin_send, average_twin_recv, twin)

    def outer_step():
        whole_wait(averages.at[pl.ds(0, 8)], average_twin_recv)

        def one(block, carry):
            at_rows = pl.ds(pl.multiple_of(block * 64, 64), 64)
            average = averages[block].astype(F32)
            moved = momentum_decay * momentum[at_rows, :] + average
            new_momentum[at_rows, :] = moved
            new_base[at_rows, :] = base[at_rows, :] - outer_rate * (average + momentum_decay * moved)
            return carry

        lax.fori_loop(0, 16, one, 0)
        pltpu.make_async_copy(new_base, base_out, out_sem.at[0]).start()
        pltpu.make_async_copy(new_momentum, momentum_out, out_sem.at[1]).start()

    def send_z(level):
        for far, by in HOPS[level]:
            block = weight.at[slice_at(far), y, x]
            send(block, block, wz_send, wz_recv.at[level], along_z(by))

    def z_event(level):
        whole_wait(weight.at[pl.ds(0, len(GROUPS[level + 1])), 0, 0], wz_recv.at[level])
        if level < 2:
            send_z(level + 1)
        send_first(level + 1)

    def send_first(group):
        for far in GROUPS[group]:
            block = weight.at[slice_at(far), y, x]
            for device in (north, south, over) if far in Y_FIRST else (right, left, across):
                send(block, block, first_send, first_recv.at[group], device)

    def send_second(group):
        whole_wait(weight.at[pl.ds(0, len(GROUPS[group])), 0, pl.ds(0, 3)], first_recv.at[group])
        for far in GROUPS[group]:
            held = weight.at[slice_at(far)]
            if far in Y_FIRST:
                block, devices = held.at[:, x], (right, left)
            else:
                block, devices = held.at[y], (north, south)
            for device in devices:
                send(block, block, second_send, second_recv.at[group], device)

    def send_third(group):
        whole_wait(weight.at[pl.ds(0, len(GROUPS[group])), pl.ds(0, 2)], second_recv.at[group])
        turns = [0, 0]
        for far in GROUPS[group]:
            held = weight.at[slice_at(far)]
            kind = int(far in Y_FIRST)
            way = turns[kind] % 2
            turns[kind] += 1
            if kind:
                block, device = held.at[:, (x + 3 - 2 * way) % 4], (right, left)[way]
            else:
                block, device = held.at[(y + 3 - 2 * way) % 4], (north, south)[way]
            send(block, block, second_send, third_recv.at[group], device)

    def normalize(part):
        def one(block, carry):
            start = pl.multiple_of(block * OWN, OWN)
            scale = jnp.concatenate([inverse[...]] * 2, axis=1)
            feature = (block % Z) * 2 + block // Z
            value = (inputs[:, pl.ds(start, OWN)].astype(F32) * scale * gains[feature]).astype(BF16)
            normed[0, block] = value[:, :128]
            normed[1, block] = value[:, 128:]
            return carry

        lax.fori_loop(part * 8, part * 8 + 8, one, 0)
        blocks = pl.ds(part * 8, 8)
        send(normed.at[1 - core, blocks], twin_normed.at[blocks], normed_send, normed_recv, twin)

    def project(group, first=0, last=None):
        if group == 0:
            whole_wait(twin_normed, normed_recv)
        if first == 0:
            whole_wait(weight.at[pl.ds(0, len(GROUPS[group])), 0], third_recv.at[group])
        total = key_total[...]
        for far in GROUPS[group][first:last]:
            at_z = slice_at(far)
            cols = jnp.concatenate([
                jnp.concatenate([held[lo * Z + at_z] for lo in range(2)], axis=1)
                for held in (normed.at[core], twin_normed)
            ], axis=0)
            parts = [
                weight[at_z, member // 2, (member % 2) * 2 + lo] for lo in range(2) for member in range(8)
            ]
            total = total + jnp.dot(cols, jnp.concatenate(parts, axis=0), preferred_element_type=F32)
        key_total[...] = total

    def send_keys():
        send(key_total.at[pl.ds(TOK, TOK)], key_twin, key_send, key_recv, twin)

    key_total[...] = jnp.zeros_like(key_total)
    plan = {
        (2, 3): ((start_weight,), (gain_event, 1)),
        (3, 1): ((z_event, 0), (gain_event, 2)),
        (3, 2): ((send_second, 0), (send_averages,)),
        (4, 0): ((z_event, 1), (send_second, 1)),
        (4, 1): ((send_third, 0), (gain_event, 3)),
        (4, 2): ((normalize, 0),),
        (4, 3): ((z_event, 2), (send_third, 1)),
        (5, 0): ((send_second, 2),),
        (5, 1): ((normalize, 1), (swap_averages,)),
        (5, 2): ((normalize, 2),),
        (5, 3): ((send_second, 3),),
        (6, 0): ((normalize, 3),),
        (6, 1): ((outer_step,),),
        (6, 2): ((send_third, 2),),
        (6, 3): ((project, 0),),
        (7, 0): ((project, 1),),
        (7, 1): ((send_third, 3),),
        (7, 2): ((project, 2, 0, 4),),
        (7, 3): ((project, 2, 4),),
        (8, 1): ((project, 3, 0, 3),),
        (8, 2): ((project, 3, 3), (send_keys,)),
    }
    for step in range(2, STEPS + 1):
        if step > 2:
            term(9 - step, 0)
            term(Z - (9 - step), 1)
            if step < 8:
                send_half(7 - step)
                if step < 7:
                    send_half(9 + step)
        for sub in range(SUBS):
            if step > 2:
                sum_unit(step, 0, (sub + SUBS // 2) % SUBS)
                sum_unit(step, 1, sub)
            for call, *args in plan.get((step, sub), ()):
                call(*args)

    term(0, 0)
    gain_col = jnp.transpose(jnp.broadcast_to(own_gain, (128, OWN)))
    dots = jnp.zeros((OWN, 128), F32)
    whole_wait(key_twin, key_recv)
    keys[...] = (key_total[:TOK] + key_twin[...]).astype(BF16)
    pltpu.make_async_copy(keys, keys_out, out_sem.at[2]).start()
    for sub in range(SUBS):
        cols = slice(sub * PART, (sub + 1) * PART)
        value = terms[0, :, cols]
        for way in range(2):
            whole_wait(landed.at[way, STEPS - 1, sub], sum_recv.at[way, STEPS - 1, sub])
            value = value + landed[way, STEPS - 1, sub].astype(F32)
        grad_weight[:, cols] = value * gain_col
        row = (new_base[pl.ds(sub, OWN, stride=4), :] * D ** (-0.5)).astype(BF16).astype(F32)
        dots = dots + row * value
    pltpu.make_async_copy(grad_weight, weight_out, out_sem.at[3]).start()
    gain_out[...] = jnp.sum(jnp.transpose(dots), axis=0, keepdims=True)

    whole_wait(twin_part, twin_send)
    whole_wait(pieces, piece_send)
    whole_wait(averages.at[pl.ds(0, 7)], average_send)
    whole_wait(averages.at[pl.ds(0, 8)], average_twin_send)
    whole_wait(halves, half_send)
    whole_wait(both.at[:, 1], up_send)
    whole_wait(gains.at[0], gain_send)
    whole_wait(gains.at[pl.ds(0, 30)], gain_z_send)
    whole_wait(twin_normed, normed_send)
    whole_wait(key_twin, key_send)
    for way in range(2):
        whole_wait(totals.at[way, 0, pl.ds(0, SUBS // 2)], sum_send.at[way, 0])
        whole_wait(totals.at[way, pl.ds(1, STEPS - 1)], sum_send.at[way, 1])
    whole_wait(weight.at[pl.ds(0, 15), 0, 0], wz_send)
    whole_wait(weight.at[pl.ds(0, 3)], first_send)
    whole_wait(weight.at[pl.ds(0, 12)], second_send)
    for index, (src, dst) in enumerate((
        (new_base, base_out), (new_momentum, momentum_out), (keys, keys_out), (grad_weight, weight_out),
    )):
        pltpu.make_async_copy(src, dst, out_sem.at[index]).wait()


def finish(*refs):
    count = len(refs) // 2
    sem = refs[-1]
    for index in range(count):
        pltpu.make_async_copy(refs[index], refs[count + index], sem.at[index]).start()
    for index in range(count):
        pltpu.make_async_copy(refs[index], refs[count + index], sem.at[index]).wait()


def shards(codes, scales, base, momentum, inputs, gain, cotangent):
    vmem = pl.BlockSpec(memory_space=pltpu.VMEM)
    hbm = pl.BlockSpec(memory_space=pl.ANY)
    dma = pltpu.SemaphoreType.DMA
    results = (
        jax.ShapeDtypeStruct((1024, 128), F32),
        jax.ShapeDtypeStruct((1024, 128), F32),
        jax.ShapeDtypeStruct((TOK, KV), BF16),
        jax.ShapeDtypeStruct((OWN, KV), F32),
        jax.ShapeDtypeStruct((1, OWN), F32),
    )
    out = pl.pallas_call(
        kernel,
        out_shape=results,
        in_specs=[hbm] * 5 + [vmem, hbm],
        out_specs=[hbm] * 4 + [vmem],
        scratch_shapes=[
            pltpu.VMEM((1024, 128), jnp.int32),
            pltpu.VMEM((16, 128), F32),
            pltpu.VMEM((1024, 128), F32),
            pltpu.VMEM((1024, 128), F32),
            pltpu.VMEM((TOK, D), BF16),
            pltpu.VMEM((TOK, KV), BF16),
            pltpu.VMEM((1024, 128), F32),
            pltpu.VMEM((1024, 128), F32),
            pltpu.VMEM((TOK, KV), BF16),
            pltpu.VMEM((OWN, KV), F32),
            pltpu.VMEM((16, 64, 128), BF16),
            pltpu.VMEM((8, 64, 128), BF16),
            pltpu.VMEM((8, 64, 128), BF16),
            pltpu.VMEM((7, 64, 128), BF16),
            pltpu.VMEM((16, 64, 128), BF16),
            pltpu.VMEM((64, 128), F32),
            pltpu.VMEM((Z, 4, 4, 16, KV), BF16),
            pltpu.VMEM((2 * Z, 1, OWN), F32),
            pltpu.VMEM((Z, TOK, OWN), BF16),
            pltpu.VMEM((SUBS, 2, TOK, PART), BF16),
            pltpu.VMEM((TOK, 128), F32),
            pltpu.VMEM((2, 2 * Z, TOK, 128), BF16),
            pltpu.VMEM((2 * Z, TOK, 128), BF16),
            pltpu.VMEM((2, STEPS, SUBS, OWN, PART), BF16),
            pltpu.VMEM((2, STEPS, SUBS, OWN, PART), BF16),
            pltpu.VMEM((2, OWN, KV), F32),
            pltpu.VMEM((2 * TOK, KV), F32),
            pltpu.VMEM((TOK, KV), F32),
            dma((9,)), dma((4,)), dma, dma, dma, dma,
            dma, dma, dma, dma,
            dma, dma((Z,)), dma, dma((SUBS,)), dma, dma, dma, dma((3,)),
            dma, dma, dma, dma, dma((2, 2)), dma((2, STEPS, SUBS)), dma, dma((3,)),
            dma, dma((4,)), dma, dma((4,)), dma((4,)),
        ],
        compiler_params=pltpu.CompilerParams(
            collective_id=0, has_side_effects=True, vmem_limit_bytes=58 * 1024 * 1024
        ),
    )(
        codes.reshape(1024, 128), scales.reshape(16, 128), base.reshape(1024, 128), momentum.reshape(1024, 128),
        inputs[0], gain, cotangent[0],
    )
    out = pl.pallas_call(
        finish, out_shape=results, in_specs=[vmem] * 5, out_specs=[hbm] * 5, scratch_shapes=[dma((5,))],
    )(*out)
    new_base, new_momentum, keys, grad_weight, grad_gain = out
    return new_base.reshape(-1), new_momentum.reshape(-1), keys[None], grad_weight[None], grad_gain


def solution(mesh):
    placed = (
        P("rep", "fsdp"),
        P("rep", "fsdp"),
        P("fsdp"),
        P("fsdp"),
        P("rep", "fsdp", None),
        P("rep", "fsdp"),
        P("rep", "fsdp", None),
    )
    return jax.shard_map(
        shards,
        mesh=mesh,
        in_specs=placed,
        out_specs=(
            P("fsdp"),
            P("fsdp"),
            P("rep", "fsdp", None),
            P("rep", "fsdp", None),
            P("rep", "fsdp"),
        ),
        check_vma=False,
    )
```

```python
import jax
import jax.numpy as jnp
from jax import lax
from jax.experimental import pallas as pl
from jax.experimental.pallas import tpu as pltpu
from jax.sharding import PartitionSpec as P

MESH = pl.DeviceIdType.MESH
F32 = jnp.float32
BF16 = jnp.bfloat16

D = 8192
KV = 512
Z = 16
OWN = 256
TOK = 128
SUBS = 4
PART = KV // SUBS
STEPS = 8
outer_rate = 0.7
momentum_decay = 0.9

HOPS = (
    ((0, 3), (0, 13), (0, 6), (0, 10)),
    ((0, 1), (0, 15), (3, 1), (-3, 15), (3, 15), (-3, 1), (6, 1), (-6, 15), (6, 15), (-6, 1), (-6, 2)),
)
GROUPS = ((0,), (3, -3, 6, -6), (1, -1, 2, -2, 4), (-4, 5, -5, 7, -7, 8))
ORDER = (8, 7, 9, 6, 10, 5, 11, 4, 12, 3, 13, 2, 14, 1, 15, 0)


def group_at(far, by):
    landed_far = (far - by + 7) % Z - 7
    return next(index for index, group in enumerate(GROUPS) if landed_far in group)


def whole_wait(ref, sem):
    pltpu.make_async_copy(ref, ref, sem).wait()


def kernel(
    codes_hbm, scales_hbm, base_hbm, momentum_hbm, inputs_hbm, gain, cotangent_hbm,
    base_out, momentum_out, keys_out, weight_out, gain_out,
    codes, scales, base, momentum, inputs, cotangent, new_base, new_momentum, keys, grad_weight,
    decoded, twin_part, pairs, pieces, averages, rows, weight, gains, halves, both, inverse,
    inverse_row, normed, twin_normed, totals, landed, terms, key_total, key_twin, key_part,
    local_sem, out_sem, twin_send, twin_recv, piece_send, piece_recv,
    average_send, average_recv, average_twin_send, average_twin_recv,
    half_send, half_recv, up_send, up_recv, row_send, row_recv, gain_z_send, gain_z_recv,
    normed_send, normed_recv, key_send, key_recv, part_send, part_recv, sum_send, sum_recv, wz_send, wz_recv,
    first_send, first_recv, second_send, second_recv, third_recv,
):
    rep = lax.axis_index("rep")
    shard = lax.axis_index("fsdp")
    core = rep % 2
    x_hi = (rep // 2) % 2
    y = rep // 4
    x_lo = shard // Z
    z = shard % Z
    x = x_hi * 2 + x_lo
    chip = rep // 2
    own = core * 8 + chip

    def at(y_to=y, x_to=x, z_to=z, core_to=core):
        return ((y_to * 2 + x_to // 2) * 2 + core_to, (x_to % 2) * Z + z_to)

    def along_z(by):
        return at(z_to=(z + by) % Z)

    def fellow(step):
        return ((chip + step) % 8) * 2 + core, shard

    ring = (along_z(1), along_z(15))
    across = at(x_to=(x + 2) % 4)
    north, south = (at(y_to=(y + by) % 4) for by in (1, 3))
    twin = at(core_to=1 - core)
    partner = at(x_to=x_hi * 2 + 1 - x_lo)

    def send(src, dst, send_sem, recv_sem, device):
        pltpu.make_async_remote_copy(
            src_ref=src, dst_ref=dst, send_sem=send_sem, recv_sem=recv_sem,
            device_id=device, device_id_type=MESH,
        ).start()

    barrier = pltpu.get_barrier_semaphore()

    def greet(step, carry):
        pl.semaphore_signal(barrier, inc=1, device_id=fellow(step), device_id_type=MESH)
        return carry

    lax.fori_loop(1, 8, greet, 0)
    near = [twin, partner] + [along_z(by) for by in (1, 15, 2, 14, 3, 13, 6, 10)]
    for device in near:
        pl.semaphore_signal(barrier, inc=1, device_id=device, device_id_type=MESH)

    def load(src, dst, index):
        pltpu.make_async_copy(src, dst, local_sem.at[index]).start()

    load(codes_hbm, codes, 5)
    load(scales_hbm, scales, 6)
    quarter = D // 4
    for index in range(4):
        cols = pl.ds(index * quarter, quarter)
        load(inputs_hbm.at[:, cols], inputs.at[:, cols], index)
    load(cotangent_hbm, cotangent, 4)
    load(base_hbm, base, 7)
    load(momentum_hbm, momentum, 8)

    entry = lax.broadcasted_iota(jnp.int32, (64, 128), 0)
    lane = lax.broadcasted_iota(jnp.int32, (64, 128), 1)
    chosen = (lane >> 1) == entry
    from_lane = lax.broadcasted_iota(jnp.int32, (128, 128), 0)
    to_lane = lax.broadcasted_iota(jnp.int32, (128, 128), 1)
    spread = ((from_lane & 1) == (to_lane >> 6)).astype(BF16)

    def decode(block, carry):
        picked = jnp.where(chosen, scales[pl.ds(block, 1), :], 0.0)
        high = picked.astype(BF16)
        low = (picked - high.astype(F32)).astype(BF16)
        scale = jnp.dot(high, spread, preferred_element_type=F32) + jnp.dot(low, spread, preferred_element_type=F32)
        code = codes[pl.ds(pl.multiple_of(block * 64, 64), 64), :]
        decoded[block] = ((code - 8).astype(F32) * scale).astype(BF16)
        return carry

    whole_wait(codes, local_sem.at[5])
    whole_wait(scales, local_sem.at[6])
    lax.fori_loop(0, 16, decode, 0)

    def squares(block, total):
        cols = inputs[:, pl.ds(pl.multiple_of(block * 512, 512), 512)].astype(F32)
        cols = cols * cols
        return total + (cols[:, :128] + cols[:, 128:256]) + (cols[:, 256:384] + cols[:, 384:])

    square = jnp.zeros((TOK, 128), F32)
    for index in range(4):
        cols = inputs.at[:, pl.ds(index * quarter, quarter)]
        whole_wait(cols, local_sem.at[index])
        square = lax.fori_loop(index * 4, index * 4 + 4, squares, square)
    inv = lax.rsqrt(jnp.sum(square, axis=1, keepdims=True) * (1.0 / D) + 1e-05)
    inverse[pl.ds(0, TOK)] = jnp.broadcast_to(inv, (TOK, 128))
    inverse_row[0] = jnp.transpose(inverse[pl.ds(0, TOK)])[:8]
    whole_wait(cotangent, local_sem.at[4])
    for sub in range(SUBS):
        both[sub, 0] = (cotangent[:, sub * PART:(sub + 1) * PART].astype(F32) * inv).astype(BF16)
    own_gain = gain[...].astype(F32)
    gains[pl.ds(z, 1)] = own_gain.reshape(1, 1, OWN)

    pl.semaphore_wait(barrier, 7 + len(near))

    def send_half(far):
        target = (z + far) % Z
        start = pl.multiple_of(((1 - x_lo) * Z + target) * OWN, OWN)
        send(inputs.at[:, pl.ds(start, OWN)], halves.at[target], half_send, half_recv.at[far], partner)

    def send_up(sub):
        send(both.at[sub, 0], both.at[sub, 1], up_send, up_recv.at[sub], partner)

    send(decoded.at[pl.ds((1 - core) * 8, 8)], twin_part, twin_send, twin_recv, twin)
    send(inverse_row.at[0], inverse_row.at[1], row_send, row_recv, partner)
    send_up(0)
    send_half(8)
    for sub in (2, 1, 3):
        send_up(sub)
    send_half(7)
    send_half(9)

    whole_wait(twin_part, twin_recv)
    for block in range(8):
        pairs[block] = (decoded[core * 8 + block].astype(F32) + twin_part[block].astype(F32)).astype(BF16)

    def send_piece(step, carry):
        send(pairs.at[(chip + step) % 8], pieces.at[step - 1], piece_send, piece_recv, fellow(step))
        return carry

    lax.fori_loop(1, 8, send_piece, 0)

    here = set()

    def need_half(far):
        if far not in here:
            whole_wait(halves.at[far], half_recv.at[far])
            here.add(far)

    def features(far):
        target = (z + far) % Z
        need_half(far)
        start = pl.multiple_of((x_lo * Z + target) * OWN, OWN)
        return jnp.concatenate([inputs[:, pl.ds(start, OWN)], halves[target]], axis=0)

    def product(cols, cotangents):
        return lax.dot_general(cols, cotangents, (((0,), (0,)), ((), ())), preferred_element_type=F32)

    def term(far, slot):
        cotangents = jnp.concatenate([both[sub].reshape(2 * TOK, PART) for sub in range(SUBS)], axis=1)
        terms[slot] = product(features(far), cotangents)

    def send_sum(step, way, sub, value):
        totals[way, step - 1, sub] = value.astype(BF16)
        send(
            totals.at[way, step - 1, sub], landed.at[way, step - 1, sub],
            sum_send.at[way, min(step - 1, 1)], sum_recv.at[way, step - 1, sub], ring[way],
        )

    def sum_unit(step, way, sub, fresh=False):
        value = terms[way, :, sub * PART:(sub + 1) * PART]
        if not fresh:
            whole_wait(landed.at[way, step - 2, sub], sum_recv.at[way, step - 2, sub])
            value = value + landed[way, step - 2, sub].astype(F32)
        send_sum(step, way, sub, value)

    cols = features(8)
    for sub in (0, 2, 1, 3):
        whole_wait(both.at[sub, 1], up_recv.at[sub])
        send_sum(1, sub // 2, sub, product(cols, both[sub].reshape(2 * TOK, PART)))
    send_half(6)
    send_half(10)

    def send_gains(level):
        for far, by in HOPS[level]:
            block = gains.at[(z + far + Z) % Z]
            send(block, block, gain_z_send, gain_z_recv.at[level], along_z(by))

    def gain_event(level):
        if level > 0:
            whole_wait(gains.at[pl.ds(0, len(HOPS[level - 1]))], gain_z_recv.at[level - 1])
        if level < 2:
            send_gains(level)

    gain_event(0)
    term(7, 0)
    term(9, 1)
    for sub in (2, 0, 3, 1):
        sum_unit(2, 1 - sub // 2, sub, fresh=True)
    send_half(5)
    send_half(11)

    mine = pl.ds(pl.multiple_of(own * 64, 64), 64)

    def slice_at(far):
        return (z + far + Z) % Z

    def start_weight():
        whole_wait(pieces, piece_recv)
        total = pairs[chip].astype(F32)
        for step in range(7):
            total = total + pieces[step].astype(F32)
        average = (total * (1.0 / 16)).astype(BF16)
        averages[own] = average
        average = average.astype(F32)
        whole_wait(base, local_sem.at[7])
        whole_wait(momentum, local_sem.at[8])
        moved = momentum_decay * momentum[mine, :] + average
        rows[...] = (base[mine, :] - outer_rate * (average + momentum_decay * moved)) * D ** (-0.5)
        for col in range(4):
            weight[z, y, x_hi, :, col * 128:(col + 1) * 128] = rows[pl.ds(col, 16, stride=4), :].astype(BF16)
        send_z(0)
        send_first(0)

    def send_averages():
        def one(step, carry):
            send(averages.at[own], averages.at[own], average_send, average_recv, fellow(step))
            return carry

        lax.fori_loop(1, 8, one, 0)

    def swap_averages():
        whole_wait(averages.at[pl.ds(0, 7)], average_recv)
        block = averages.at[pl.ds(core * 8, 8)]
        send(block, block, average_twin_send, average_twin_recv, twin)

    def outer_step():
        whole_wait(averages.at[pl.ds(0, 8)], average_twin_recv)

        def one(block, carry):
            at_rows = pl.ds(pl.multiple_of(block * 64, 64), 64)
            average = averages[block].astype(F32)
            moved = momentum_decay * momentum[at_rows, :] + average
            new_momentum[at_rows, :] = moved
            new_base[at_rows, :] = base[at_rows, :] - outer_rate * (average + momentum_decay * moved)
            return carry

        lax.fori_loop(0, 16, one, 0)
        pltpu.make_async_copy(new_base, base_out, out_sem.at[0]).start()
        pltpu.make_async_copy(new_momentum, momentum_out, out_sem.at[1]).start()

    def send_z(level):
        for far, by in HOPS[level]:
            block = weight.at[slice_at(far), y, x_hi]
            send(block, block, wz_send, wz_recv.at[group_at(far, by)], along_z(by))

    def z_event(group):
        whole_wait(weight.at[pl.ds(0, len(GROUPS[group])), 0, 0], wz_recv.at[group])
        if group == 1:
            send_z(1)
        send_first(group)

    def send_first(group):
        for far in GROUPS[group]:
            block = weight.at[slice_at(far), y, x_hi]
            send(block, block, first_send, first_recv.at[group], across)

    def send_second(group):
        whole_wait(weight.at[pl.ds(0, len(GROUPS[group])), 0, 0], first_recv.at[group])
        for far in GROUPS[group]:
            block = weight.at[slice_at(far), y]
            for device in (north, south):
                send(block, block, second_send, second_recv.at[group], device)

    def send_third(group):
        whole_wait(weight.at[pl.ds(0, len(GROUPS[group])), pl.ds(0, 2)], second_recv.at[group])
        for turn, far in enumerate(GROUPS[group]):
            way = turn % 2
            block = weight.at[slice_at(far), (y + 3 - 2 * way) % 4]
            send(block, block, second_send, third_recv.at[group], (north, south)[way])

    def normalize(part):
        if part == 0:
            whole_wait(inverse_row.at[1], row_recv)
            inverse[pl.ds(TOK, TOK)] = jnp.transpose(jnp.broadcast_to(inverse_row[1, 0:1], (128, TOK)))
        scale = jnp.concatenate([inverse[...]] * 2, axis=1)
        for place in range(part * 4, part * 4 + 4):
            value = (features(ORDER[place]).astype(F32) * scale * gains[slice_at(ORDER[place])]).astype(BF16)
            normed[0, place] = value[:, :128]
            normed[1, place] = value[:, 128:]
        places = pl.ds(part * 4, 4)
        send(normed.at[1 - core, places], twin_normed.at[places], normed_send, normed_recv, twin)

    def project(half):
        if half == 0:
            whole_wait(twin_normed, normed_recv)
            for group in range(len(GROUPS)):
                whole_wait(weight.at[pl.ds(0, len(GROUPS[group])), 0], third_recv.at[group])
        places = range(half * 8, half * 8 + 8)
        cols = jnp.concatenate([
            jnp.concatenate([normed[core, place] for place in places], axis=1),
            jnp.concatenate([twin_normed[place] for place in places], axis=1),
        ], axis=0)
        held = jnp.concatenate([weight[slice_at(ORDER[place])].reshape(128, KV) for place in places], axis=0)
        value = jnp.dot(cols, held, preferred_element_type=F32)
        key_total[...] = value if half == 0 else key_total[...] + value

    def send_keys():
        send(key_total.at[pl.ds(2 * TOK, 2 * TOK)], key_twin, key_send, key_recv, twin)

    def swap_keys():
        whole_wait(key_twin, key_recv)
        key_part[0] = (key_total[pl.ds(TOK, TOK)] + key_twin[pl.ds(TOK, TOK)]).astype(BF16)
        send(key_part.at[0], key_part.at[1], part_send, part_recv, partner)

    for sub in (0, 2):
        sum_unit(2, sub // 2, sub)
    start_weight()
    for sub in (1, 3):
        sum_unit(2, sub // 2, sub)
    plan = {
        (2, 3): ((gain_event, 1),),
        (3, 1): ((send_averages,),),
        (3, 2): ((z_event, 1),),
        (3, 3): ((send_second, 0), (gain_event, 2)),
        (4, 1): ((send_third, 0),),
        (4, 2): ((send_second, 1),),
        (4, 3): ((z_event, 2),),
        (5, 0): ((z_event, 3),),
        (5, 1): ((normalize, 0), (swap_averages,)),
        (5, 2): ((send_second, 2), (send_third, 1)),
        (5, 3): ((send_second, 3),),
        (6, 0): ((normalize, 1),),
        (6, 1): ((outer_step,),),
        (6, 2): ((send_third, 2), (normalize, 2)),
        (6, 3): ((send_third, 3),),
        (7, 0): ((normalize, 3),),
        (7, 3): ((project, 0),),
        (8, 0): ((project, 1), (send_keys,)),
        (8, 3): ((swap_keys,),),
    }
    for step in range(2, STEPS + 1):
        if step > 2:
            term(9 - step, 0)
            term(Z - (9 - step), 1)
            for far in ORDER[3 * step - 2:3 * step + 1]:
                send_half(far)
        for sub in range(SUBS):
            if step > 2:
                sum_unit(step, 0, (sub + SUBS // 2) % SUBS)
                sum_unit(step, 1, sub)
            for call, *args in plan.get((step, sub), ()):
                call(*args)

    term(0, 0)
    gain_col = jnp.transpose(jnp.broadcast_to(own_gain, (128, OWN)))
    dots = jnp.zeros((OWN, 128), F32)
    whole_wait(key_part.at[1], part_recv)
    keys[...] = (key_total[:TOK] + key_twin[:TOK] + key_part[1].astype(F32)).astype(BF16)
    pltpu.make_async_copy(keys, keys_out, out_sem.at[2]).start()
    for sub in (0, 2, 1, 3):
        cols = slice(sub * PART, (sub + 1) * PART)
        value = terms[0, :, cols]
        for way in range(2):
            whole_wait(landed.at[way, STEPS - 1, sub], sum_recv.at[way, STEPS - 1, sub])
            value = value + landed[way, STEPS - 1, sub].astype(F32)
        grad_weight[:, cols] = value * gain_col
        row = (new_base[pl.ds(sub, OWN, stride=4), :] * D ** (-0.5)).astype(BF16).astype(F32)
        dots = dots + row * value
        pltpu.make_async_copy(grad_weight.at[:, cols], weight_out.at[:, cols], out_sem.at[3 + sub]).start()
    gain_out[...] = jnp.sum(jnp.transpose(dots), axis=0, keepdims=True)

    whole_wait(twin_part, twin_send)
    whole_wait(pieces, piece_send)
    whole_wait(averages.at[pl.ds(0, 7)], average_send)
    whole_wait(averages.at[pl.ds(0, 8)], average_twin_send)
    whole_wait(halves, half_send)
    whole_wait(both.at[:, 1], up_send)
    whole_wait(inverse_row.at[1], row_send)
    whole_wait(gains.at[pl.ds(0, 15)], gain_z_send)
    whole_wait(twin_normed, normed_send)
    whole_wait(key_twin, key_send)
    whole_wait(key_part.at[1], part_send)
    for way in range(2):
        whole_wait(totals.at[way, 0, pl.ds(0, SUBS // 2)], sum_send.at[way, 0])
        whole_wait(totals.at[way, pl.ds(1, STEPS - 1)], sum_send.at[way, 1])
    whole_wait(weight.at[pl.ds(0, 15), 0, 0], wz_send)
    whole_wait(weight.at[pl.ds(0, 2)], first_send)
    whole_wait(weight.at[pl.ds(0, 12)], second_send)
    for index, (src, dst) in enumerate((
        (new_base, base_out), (new_momentum, momentum_out), (keys, keys_out),
    )):
        pltpu.make_async_copy(src, dst, out_sem.at[index]).wait()
    for sub in range(SUBS):
        cols = slice(sub * PART, (sub + 1) * PART)
        pltpu.make_async_copy(grad_weight.at[:, cols], weight_out.at[:, cols], out_sem.at[3 + sub]).wait()


def finish(*refs):
    sources, results, held, sem = refs[:5], refs[5:10], refs[10:15], refs[15]
    inward = [pltpu.make_async_copy(sources[index], held[index], sem.at[0, index]) for index in range(5)]
    outward = [pltpu.make_async_copy(held[index], results[index], sem.at[1, index]) for index in range(5)]
    for copy in inward:
        copy.start()
    for index in range(5):
        inward[index].wait()
        outward[index].start()
    for copy in outward:
        copy.wait()


def shards(codes, scales, base, momentum, inputs, gain, cotangent):
    vmem = pl.BlockSpec(memory_space=pltpu.VMEM)
    hbm = pl.BlockSpec(memory_space=pl.ANY)
    dma = pltpu.SemaphoreType.DMA
    results = (
        jax.ShapeDtypeStruct((1024, 128), F32),
        jax.ShapeDtypeStruct((1024, 128), F32),
        jax.ShapeDtypeStruct((TOK, KV), BF16),
        jax.ShapeDtypeStruct((OWN, KV), F32),
        jax.ShapeDtypeStruct((1, OWN), F32),
    )
    out = pl.pallas_call(
        kernel,
        out_shape=results,
        in_specs=[hbm] * 5 + [vmem, hbm],
        out_specs=[hbm] * 4 + [vmem],
        scratch_shapes=[
            pltpu.VMEM((1024, 128), jnp.int32),
            pltpu.VMEM((16, 128), F32),
            pltpu.VMEM((1024, 128), F32),
            pltpu.VMEM((1024, 128), F32),
            pltpu.VMEM((TOK, D), BF16),
            pltpu.VMEM((TOK, KV), BF16),
            pltpu.VMEM((1024, 128), F32),
            pltpu.VMEM((1024, 128), F32),
            pltpu.VMEM((TOK, KV), BF16),
            pltpu.VMEM((OWN, KV), F32),
            pltpu.VMEM((16, 64, 128), BF16),
            pltpu.VMEM((8, 64, 128), BF16),
            pltpu.VMEM((8, 64, 128), BF16),
            pltpu.VMEM((7, 64, 128), BF16),
            pltpu.VMEM((16, 64, 128), BF16),
            pltpu.VMEM((64, 128), F32),
            pltpu.VMEM((Z, 4, 2, 16, KV), BF16),
            pltpu.VMEM((Z, 1, OWN), F32),
            pltpu.VMEM((Z, TOK, OWN), BF16),
            pltpu.VMEM((SUBS, 2, TOK, PART), BF16),
            pltpu.VMEM((2 * TOK, 128), F32),
            pltpu.VMEM((2, 8, TOK), F32),
            pltpu.VMEM((2, Z, 2 * TOK, 128), BF16),
            pltpu.VMEM((Z, 2 * TOK, 128), BF16),
            pltpu.VMEM((2, STEPS, SUBS, OWN, PART), BF16),
            pltpu.VMEM((2, STEPS, SUBS, OWN, PART), BF16),
            pltpu.VMEM((2, OWN, KV), F32),
            pltpu.VMEM((4 * TOK, KV), F32),
            pltpu.VMEM((2 * TOK, KV), F32),
            pltpu.VMEM((2, TOK, KV), BF16),
            dma((9,)), dma((3 + SUBS,)), dma, dma, dma, dma,
            dma, dma, dma, dma,
            dma, dma((Z,)), dma, dma((SUBS,)), dma, dma, dma, dma((2,)),
            dma, dma, dma, dma, dma, dma, dma((2, 2)), dma((2, STEPS, SUBS)), dma, dma((4,)),
            dma, dma((4,)), dma, dma((4,)), dma((4,)),
        ],
        compiler_params=pltpu.CompilerParams(
            collective_id=0, has_side_effects=True, vmem_limit_bytes=58 * 1024 * 1024
        ),
    )(
        codes.reshape(1024, 128), scales.reshape(16, 128), base.reshape(1024, 128), momentum.reshape(1024, 128),
        inputs[0], gain, cotangent[0],
    )
    out = pl.pallas_call(
        finish, out_shape=results, in_specs=[hbm] * 5, out_specs=[hbm] * 5,
        scratch_shapes=[pltpu.VMEM(result.shape, result.dtype) for result in results] + [dma((2, 5))],
        compiler_params=pltpu.CompilerParams(vmem_limit_bytes=58 * 1024 * 1024),
    )(*out)
    new_base, new_momentum, keys, grad_weight, grad_gain = out
    return new_base.reshape(-1), new_momentum.reshape(-1), keys[None], grad_weight[None], grad_gain


def solution(mesh):
    placed = (
        P("rep", "fsdp"),
        P("rep", "fsdp"),
        P("fsdp"),
        P("fsdp"),
        P("rep", "fsdp", None),
        P("rep", "fsdp"),
        P("rep", "fsdp", None),
    )
    return jax.shard_map(
        shards,
        mesh=mesh,
        in_specs=placed,
        out_specs=(
            P("fsdp"),
            P("fsdp"),
            P("rep", "fsdp", None),
            P("rep", "fsdp", None),
            P("rep", "fsdp"),
        ),
        check_vma=False,
    )
```

```python
import jax
import jax.numpy as jnp
from jax import lax
from jax.experimental import pallas as pl
from jax.experimental.pallas import tpu as pltpu
from jax.sharding import PartitionSpec as P

MESH = pl.DeviceIdType.MESH
F32 = jnp.float32
BF16 = jnp.bfloat16

D = 8192
KV = 512
Z = 16
OWN = 256
TOK = 128
SUBS = 4
PART = KV // SUBS
STEPS = 8
outer_rate = 0.7
momentum_decay = 0.9

HOPS = (
    ((0, 3), (0, 13), (0, 6), (0, 10)),
    ((0, 1), (0, 15), (3, 1), (-3, 15), (3, 15), (-3, 1), (6, 1), (-6, 15), (6, 15), (-6, 1), (-6, 2)),
)
GROUPS = ((0,), (3, -3, 6, -6), (1, -1, 2, -2, 4), (-4, 5, -5, 7, -7, 8))
ORDER = (8, 7, 9, 6, 10, 5, 11, 4, 12, 3, 13, 2, 14, 1, 15, 0)


def group_at(far, by):
    landed_far = (far - by + 7) % Z - 7
    return next(index for index, group in enumerate(GROUPS) if landed_far in group)


def whole_wait(ref, sem):
    pltpu.make_async_copy(ref, ref, sem).wait()


def kernel(
    codes_hbm, scales_hbm, base_hbm, momentum_hbm, inputs_hbm, gain, cotangent_hbm,
    base_out, momentum_out, keys_out, weight_out, gain_out,
    codes, scales, base, momentum, inputs, cotangent, new_base, new_momentum, keys, grad_weight,
    decoded, twin_part, pairs, pieces, averages, rows, weight, gains, halves, both, inverse,
    inverse_row, normed, twin_normed, totals, landed, terms, key_total, key_twin, key_part,
    local_sem, out_sem, twin_send, twin_recv, piece_send, piece_recv,
    average_send, average_recv, average_twin_send, average_twin_recv,
    half_send, half_recv, up_send, up_recv, row_send, row_recv, gain_z_send, gain_z_recv,
    normed_send, normed_recv, key_send, key_recv, part_send, part_recv, sum_send, sum_recv, wz_send, wz_recv,
    first_send, first_recv, second_send, second_recv, third_recv,
):
    rep = lax.axis_index("rep")
    shard = lax.axis_index("fsdp")
    core = rep % 2
    x_hi = (rep // 2) % 2
    y = rep // 4
    x_lo = shard // Z
    z = shard % Z
    x = x_hi * 2 + x_lo
    chip = rep // 2
    own = core * 8 + chip

    def at(y_to=y, x_to=x, z_to=z, core_to=core):
        return ((y_to * 2 + x_to // 2) * 2 + core_to, (x_to % 2) * Z + z_to)

    def along_z(by):
        return at(z_to=(z + by) % Z)

    def fellow(step):
        return ((chip + step) % 8) * 2 + core, shard

    ring = (along_z(1), along_z(15))
    across = at(x_to=(x + 2) % 4)
    north, south = (at(y_to=(y + by) % 4) for by in (1, 3))
    twin = at(core_to=1 - core)
    partner = at(x_to=x_hi * 2 + 1 - x_lo)

    def send(src, dst, send_sem, recv_sem, device):
        pltpu.make_async_remote_copy(
            src_ref=src, dst_ref=dst, send_sem=send_sem, recv_sem=recv_sem,
            device_id=device, device_id_type=MESH,
        ).start()

    barrier = pltpu.get_barrier_semaphore()

    def greet(step, carry):
        pl.semaphore_signal(barrier, inc=1, device_id=fellow(step), device_id_type=MESH)
        return carry

    lax.fori_loop(1, 8, greet, 0)
    near = [twin, partner] + [along_z(by) for by in (1, 15, 2, 14, 3, 13, 6, 10)]
    for device in near:
        pl.semaphore_signal(barrier, inc=1, device_id=device, device_id_type=MESH)

    def load(src, dst, index):
        pltpu.make_async_copy(src, dst, local_sem.at[index]).start()

    load(codes_hbm, codes, 5)
    load(scales_hbm, scales, 6)
    quarter = D // 4
    for index in range(4):
        cols = pl.ds(index * quarter, quarter)
        load(inputs_hbm.at[:, cols], inputs.at[:, cols], index)
    load(cotangent_hbm, cotangent, 4)
    load(base_hbm, base, 7)
    load(momentum_hbm, momentum, 8)

    entry = lax.broadcasted_iota(jnp.int32, (64, 128), 0)
    lane = lax.broadcasted_iota(jnp.int32, (64, 128), 1)
    chosen = (lane >> 1) == entry
    from_lane = lax.broadcasted_iota(jnp.int32, (128, 128), 0)
    to_lane = lax.broadcasted_iota(jnp.int32, (128, 128), 1)
    spread = ((from_lane & 1) == (to_lane >> 6)).astype(BF16)

    def decode(block, carry):
        picked = jnp.where(chosen, scales[pl.ds(block, 1), :], 0.0)
        high = picked.astype(BF16)
        low = (picked - high.astype(F32)).astype(BF16)
        scale = jnp.dot(high, spread, preferred_element_type=F32) + jnp.dot(low, spread, preferred_element_type=F32)
        code = codes[pl.ds(pl.multiple_of(block * 64, 64), 64), :]
        decoded[block] = ((code - 8).astype(F32) * scale).astype(BF16)
        return carry

    whole_wait(codes, local_sem.at[5])
    whole_wait(scales, local_sem.at[6])
    lax.fori_loop(0, 16, decode, 0)

    def squares(block, total):
        cols = inputs[:, pl.ds(pl.multiple_of(block * 512, 512), 512)].astype(F32)
        cols = cols * cols
        return total + (cols[:, :128] + cols[:, 128:256]) + (cols[:, 256:384] + cols[:, 384:])

    square = jnp.zeros((TOK, 128), F32)
    for index in range(4):
        cols = inputs.at[:, pl.ds(index * quarter, quarter)]
        whole_wait(cols, local_sem.at[index])
        square = lax.fori_loop(index * 4, index * 4 + 4, squares, square)
    inv = lax.rsqrt(jnp.sum(square, axis=1, keepdims=True) * (1.0 / D) + 1e-05)
    inverse[pl.ds(0, TOK)] = jnp.broadcast_to(inv, (TOK, 128))
    inverse_row[0] = jnp.transpose(inverse[pl.ds(0, TOK)])[:8]
    whole_wait(cotangent, local_sem.at[4])
    for sub in range(SUBS):
        both[sub, 0] = (cotangent[:, sub * PART:(sub + 1) * PART].astype(F32) * inv).astype(BF16)
    own_gain = gain[...].astype(F32)
    gains[pl.ds(z, 1)] = own_gain.reshape(1, 1, OWN)

    pl.semaphore_wait(barrier, 7 + len(near))

    def send_half(far):
        target = (z + far) % Z
        start = pl.multiple_of(((1 - x_lo) * Z + target) * OWN, OWN)
        send(inputs.at[:, pl.ds(start, OWN)], halves.at[target], half_send, half_recv.at[far], partner)

    def send_up(sub):
        send(both.at[sub, 0], both.at[sub, 1], up_send, up_recv.at[sub], partner)

    send(decoded.at[pl.ds((1 - core) * 8, 8)], twin_part, twin_send, twin_recv, twin)
    send(inverse_row.at[0], inverse_row.at[1], row_send, row_recv, partner)
    send_up(0)
    send_half(8)
    for sub in (2, 1, 3):
        send_up(sub)
    send_half(7)
    send_half(9)

    whole_wait(twin_part, twin_recv)
    for block in range(8):
        pairs[block] = (decoded[core * 8 + block].astype(F32) + twin_part[block].astype(F32)).astype(BF16)

    def send_piece(step, carry):
        send(pairs.at[(chip + step) % 8], pieces.at[step - 1], piece_send, piece_recv, fellow(step))
        return carry

    lax.fori_loop(1, 8, send_piece, 0)

    here = set()

    def need_half(far):
        if far not in here:
            whole_wait(halves.at[far], half_recv.at[far])
            here.add(far)

    def features(far):
        target = (z + far) % Z
        need_half(far)
        start = pl.multiple_of((x_lo * Z + target) * OWN, OWN)
        return jnp.concatenate([inputs[:, pl.ds(start, OWN)], halves[target]], axis=0)

    def product(cols, cotangents):
        return lax.dot_general(cols, cotangents, (((0,), (0,)), ((), ())), preferred_element_type=F32)

    def term(far, slot):
        cotangents = jnp.concatenate([both[sub].reshape(2 * TOK, PART) for sub in range(SUBS)], axis=1)
        terms[slot] = product(features(far), cotangents)

    def send_sum(step, way, sub, value):
        totals[way, step - 1, sub] = value.astype(BF16)
        send(
            totals.at[way, step - 1, sub], landed.at[way, step - 1, sub],
            sum_send.at[way, min(step - 1, 1)], sum_recv.at[way, step - 1, sub], ring[way],
        )

    def sum_unit(step, way, sub, fresh=False):
        value = terms[way, :, sub * PART:(sub + 1) * PART]
        if not fresh:
            whole_wait(landed.at[way, step - 2, sub], sum_recv.at[way, step - 2, sub])
            value = value + landed[way, step - 2, sub].astype(F32)
        send_sum(step, way, sub, value)

    cols = features(8)
    for sub in (0, 2, 1, 3):
        whole_wait(both.at[sub, 1], up_recv.at[sub])
        send_sum(1, sub // 2, sub, product(cols, both[sub].reshape(2 * TOK, PART)))
    send_half(6)
    send_half(10)

    def send_gains(level):
        for far, by in HOPS[level]:
            block = gains.at[(z + far + Z) % Z]
            send(block, block, gain_z_send, gain_z_recv.at[level], along_z(by))

    def gain_event(level):
        if level > 0:
            whole_wait(gains.at[pl.ds(0, len(HOPS[level - 1]))], gain_z_recv.at[level - 1])
        if level < 2:
            send_gains(level)

    gain_event(0)
    term(7, 0)
    term(9, 1)
    for sub in (2, 0, 3, 1):
        sum_unit(2, 1 - sub // 2, sub, fresh=True)
    send_half(5)
    send_half(11)

    mine = pl.ds(pl.multiple_of(own * 64, 64), 64)

    def slice_at(far):
        return (z + far + Z) % Z

    def start_weight():
        whole_wait(pieces, piece_recv)
        total = pairs[chip].astype(F32)
        for step in range(7):
            total = total + pieces[step].astype(F32)
        average = (total * (1.0 / 16)).astype(BF16)
        averages[own] = average
        average = average.astype(F32)
        whole_wait(base, local_sem.at[7])
        whole_wait(momentum, local_sem.at[8])
        moved = momentum_decay * momentum[mine, :] + average
        rows[...] = (base[mine, :] - outer_rate * (average + momentum_decay * moved)) * D ** (-0.5)
        for col in range(4):
            weight[z, y, x_hi, :, col * 128:(col + 1) * 128] = rows[pl.ds(col, 16, stride=4), :].astype(BF16)
        send_z(0)
        send_first(0)

    def send_averages():
        def one(step, carry):
            send(averages.at[own], averages.at[own], average_send, average_recv, fellow(step))
            return carry

        lax.fori_loop(1, 8, one, 0)

    def swap_averages():
        whole_wait(averages.at[pl.ds(0, 7)], average_recv)
        block = averages.at[pl.ds(core * 8, 8)]
        send(block, block, average_twin_send, average_twin_recv, twin)

    def outer_step():
        whole_wait(averages.at[pl.ds(0, 8)], average_twin_recv)

        def one(block, carry):
            at_rows = pl.ds(pl.multiple_of(block * 64, 64), 64)
            average = averages[block].astype(F32)
            moved = momentum_decay * momentum[at_rows, :] + average
            new_momentum[at_rows, :] = moved
            new_base[at_rows, :] = base[at_rows, :] - outer_rate * (average + momentum_decay * moved)
            return carry

        lax.fori_loop(0, 16, one, 0)
        pltpu.make_async_copy(new_base, base_out, out_sem.at[0]).start()
        pltpu.make_async_copy(new_momentum, momentum_out, out_sem.at[1]).start()

    def send_z(level):
        for far, by in HOPS[level]:
            block = weight.at[slice_at(far), y, x_hi]
            send(block, block, wz_send, wz_recv.at[group_at(far, by)], along_z(by))

    def z_event(group):
        whole_wait(weight.at[pl.ds(0, len(GROUPS[group])), 0, 0], wz_recv.at[group])
        if group == 1:
            send_z(1)
        send_first(group)

    def send_first(group):
        for far in GROUPS[group]:
            block = weight.at[slice_at(far), y, x_hi]
            send(block, block, first_send, first_recv.at[group], across)

    def send_second(group):
        whole_wait(weight.at[pl.ds(0, len(GROUPS[group])), 0, 0], first_recv.at[group])
        for far in GROUPS[group]:
            block = weight.at[slice_at(far), y]
            for device in (north, south):
                send(block, block, second_send, second_recv.at[group], device)

    def send_third(group):
        whole_wait(weight.at[pl.ds(0, len(GROUPS[group])), pl.ds(0, 2)], second_recv.at[group])
        for turn, far in enumerate(GROUPS[group]):
            way = turn % 2
            block = weight.at[slice_at(far), (y + 3 - 2 * way) % 4]
            send(block, block, second_send, third_recv.at[group], (north, south)[way])

    def normalize(part):
        if part == 0:
            whole_wait(inverse_row.at[1], row_recv)
            inverse[pl.ds(TOK, TOK)] = jnp.transpose(jnp.broadcast_to(inverse_row[1, 0:1], (128, TOK)))
        scale = jnp.concatenate([inverse[...]] * 2, axis=1)
        for place in range(part * 4, part * 4 + 4):
            value = (features(ORDER[place]).astype(F32) * scale * gains[slice_at(ORDER[place])]).astype(BF16)
            normed[0, place] = value[:, :128]
            normed[1, place] = value[:, 128:]
        places = pl.ds(part * 4, 4)
        send(normed.at[1 - core, places], twin_normed.at[places], normed_send, normed_recv, twin)

    def project(half):
        if half == 0:
            whole_wait(twin_normed, normed_recv)
            for group in range(len(GROUPS)):
                whole_wait(weight.at[pl.ds(0, len(GROUPS[group])), 0], third_recv.at[group])
        places = range(half * 8, half * 8 + 8)
        cols = jnp.concatenate([
            jnp.concatenate([normed[core, place] for place in places], axis=1),
            jnp.concatenate([twin_normed[place] for place in places], axis=1),
        ], axis=0)
        held = jnp.concatenate([weight[slice_at(ORDER[place])].reshape(128, KV) for place in places], axis=0)
        value = jnp.dot(cols, held, preferred_element_type=F32)
        key_total[...] = value if half == 0 else key_total[...] + value

    def send_keys():
        send(key_total.at[pl.ds(2 * TOK, 2 * TOK)], key_twin, key_send, key_recv, twin)

    def swap_keys():
        whole_wait(key_twin, key_recv)
        key_part[0] = (key_total[pl.ds(TOK, TOK)] + key_twin[pl.ds(TOK, TOK)]).astype(BF16)
        send(key_part.at[0], key_part.at[1], part_send, part_recv, partner)

    for sub in (0, 2):
        sum_unit(2, sub // 2, sub)
    start_weight()
    for sub in (1, 3):
        sum_unit(2, sub // 2, sub)
    plan = {
        (2, 3): ((gain_event, 1),),
        (3, 1): ((z_event, 1),),
        (3, 2): ((send_averages,),),
        (3, 3): ((send_second, 0), (gain_event, 2)),
        (4, 1): ((send_third, 0),),
        (4, 2): ((send_second, 1),),
        (4, 3): ((z_event, 2),),
        (5, 0): ((z_event, 3),),
        (5, 1): ((normalize, 0), (swap_averages,)),
        (5, 2): ((send_second, 2), (send_third, 1)),
        (5, 3): ((send_second, 3),),
        (6, 0): ((normalize, 1),),
        (6, 1): ((outer_step,),),
        (6, 2): ((send_third, 2), (normalize, 2)),
        (6, 3): ((send_third, 3),),
        (7, 0): ((normalize, 3),),
        (7, 3): ((project, 0),),
        (8, 0): ((project, 1), (send_keys,)),
        (8, 3): ((swap_keys,),),
    }
    for step in range(2, STEPS + 1):
        if step > 2:
            term(9 - step, 0)
            term(Z - (9 - step), 1)
            for far in ORDER[3 * step - 2:3 * step + 1]:
                send_half(far)
        for sub in range(SUBS):
            if step > 2:
                sum_unit(step, 0, (sub + SUBS // 2) % SUBS)
                sum_unit(step, 1, sub)
            for call, *args in plan.get((step, sub), ()):
                call(*args)

    term(0, 0)
    gain_col = jnp.transpose(jnp.broadcast_to(own_gain, (128, OWN)))
    dots = jnp.zeros((OWN, 128), F32)
    whole_wait(key_part.at[1], part_recv)
    keys[...] = (key_total[:TOK] + key_twin[:TOK] + key_part[1].astype(F32)).astype(BF16)
    pltpu.make_async_copy(keys, keys_out, out_sem.at[2]).start()
    for sub in (0, 2, 1, 3):
        cols = slice(sub * PART, (sub + 1) * PART)
        value = terms[0, :, cols]
        for way in range(2):
            whole_wait(landed.at[way, STEPS - 1, sub], sum_recv.at[way, STEPS - 1, sub])
            value = value + landed[way, STEPS - 1, sub].astype(F32)
        grad_weight[:, cols] = value * gain_col
        row = (new_base[pl.ds(sub, OWN, stride=4), :] * D ** (-0.5)).astype(BF16).astype(F32)
        dots = dots + row * value
        pltpu.make_async_copy(grad_weight.at[:, cols], weight_out.at[:, cols], out_sem.at[3 + sub]).start()
    gain_out[...] = jnp.sum(jnp.transpose(dots), axis=0, keepdims=True)

    whole_wait(twin_part, twin_send)
    whole_wait(pieces, piece_send)
    whole_wait(averages.at[pl.ds(0, 7)], average_send)
    whole_wait(averages.at[pl.ds(0, 8)], average_twin_send)
    whole_wait(halves, half_send)
    whole_wait(both.at[:, 1], up_send)
    whole_wait(inverse_row.at[1], row_send)
    whole_wait(gains.at[pl.ds(0, 15)], gain_z_send)
    whole_wait(twin_normed, normed_send)
    whole_wait(key_twin, key_send)
    whole_wait(key_part.at[1], part_send)
    for way in range(2):
        whole_wait(totals.at[way, 0, pl.ds(0, SUBS // 2)], sum_send.at[way, 0])
        whole_wait(totals.at[way, pl.ds(1, STEPS - 1)], sum_send.at[way, 1])
    whole_wait(weight.at[pl.ds(0, 15), 0, 0], wz_send)
    whole_wait(weight.at[pl.ds(0, 2)], first_send)
    whole_wait(weight.at[pl.ds(0, 12)], second_send)
    for index, (src, dst) in enumerate((
        (new_base, base_out), (new_momentum, momentum_out), (keys, keys_out),
    )):
        pltpu.make_async_copy(src, dst, out_sem.at[index]).wait()
    for sub in range(SUBS):
        cols = slice(sub * PART, (sub + 1) * PART)
        pltpu.make_async_copy(grad_weight.at[:, cols], weight_out.at[:, cols], out_sem.at[3 + sub]).wait()


def finish(*refs):
    sources, results, held, sem = refs[:5], refs[5:10], refs[10:15], refs[15]
    inward = [pltpu.make_async_copy(sources[index], held[index], sem.at[0, index]) for index in range(5)]
    outward = [pltpu.make_async_copy(held[index], results[index], sem.at[1, index]) for index in range(5)]
    for copy in inward:
        copy.start()
    for index in range(5):
        inward[index].wait()
        outward[index].start()
    for copy in outward:
        copy.wait()


def shards(codes, scales, base, momentum, inputs, gain, cotangent):
    vmem = pl.BlockSpec(memory_space=pltpu.VMEM)
    hbm = pl.BlockSpec(memory_space=pl.ANY)
    dma = pltpu.SemaphoreType.DMA
    results = (
        jax.ShapeDtypeStruct((1024, 128), F32),
        jax.ShapeDtypeStruct((1024, 128), F32),
        jax.ShapeDtypeStruct((TOK, KV), BF16),
        jax.ShapeDtypeStruct((OWN, KV), F32),
        jax.ShapeDtypeStruct((1, OWN), F32),
    )
    out = pl.pallas_call(
        kernel,
        out_shape=results,
        in_specs=[hbm] * 5 + [vmem, hbm],
        out_specs=[hbm] * 4 + [vmem],
        scratch_shapes=[
            pltpu.VMEM((1024, 128), jnp.int32),
            pltpu.VMEM((16, 128), F32),
            pltpu.VMEM((1024, 128), F32),
            pltpu.VMEM((1024, 128), F32),
            pltpu.VMEM((TOK, D), BF16),
            pltpu.VMEM((TOK, KV), BF16),
            pltpu.VMEM((1024, 128), F32),
            pltpu.VMEM((1024, 128), F32),
            pltpu.VMEM((TOK, KV), BF16),
            pltpu.VMEM((OWN, KV), F32),
            pltpu.VMEM((16, 64, 128), BF16),
            pltpu.VMEM((8, 64, 128), BF16),
            pltpu.VMEM((8, 64, 128), BF16),
            pltpu.VMEM((7, 64, 128), BF16),
            pltpu.VMEM((16, 64, 128), BF16),
            pltpu.VMEM((64, 128), F32),
            pltpu.VMEM((Z, 4, 2, 16, KV), BF16),
            pltpu.VMEM((Z, 1, OWN), F32),
            pltpu.VMEM((Z, TOK, OWN), BF16),
            pltpu.VMEM((SUBS, 2, TOK, PART), BF16),
            pltpu.VMEM((2 * TOK, 128), F32),
            pltpu.VMEM((2, 8, TOK), F32),
            pltpu.VMEM((2, Z, 2 * TOK, 128), BF16),
            pltpu.VMEM((Z, 2 * TOK, 128), BF16),
            pltpu.VMEM((2, STEPS, SUBS, OWN, PART), BF16),
            pltpu.VMEM((2, STEPS, SUBS, OWN, PART), BF16),
            pltpu.VMEM((2, OWN, KV), F32),
            pltpu.VMEM((4 * TOK, KV), F32),
            pltpu.VMEM((2 * TOK, KV), F32),
            pltpu.VMEM((2, TOK, KV), BF16),
            dma((9,)), dma((3 + SUBS,)), dma, dma, dma, dma,
            dma, dma, dma, dma,
            dma, dma((Z,)), dma, dma((SUBS,)), dma, dma, dma, dma((2,)),
            dma, dma, dma, dma, dma, dma, dma((2, 2)), dma((2, STEPS, SUBS)), dma, dma((4,)),
            dma, dma((4,)), dma, dma((4,)), dma((4,)),
        ],
        compiler_params=pltpu.CompilerParams(
            collective_id=0, has_side_effects=True, vmem_limit_bytes=58 * 1024 * 1024
        ),
    )(
        codes.reshape(1024, 128), scales.reshape(16, 128), base.reshape(1024, 128), momentum.reshape(1024, 128),
        inputs[0], gain, cotangent[0],
    )
    out = pl.pallas_call(
        finish, out_shape=results, in_specs=[hbm] * 5, out_specs=[hbm] * 5,
        scratch_shapes=[pltpu.VMEM(result.shape, result.dtype) for result in results] + [dma((2, 5))],
        compiler_params=pltpu.CompilerParams(vmem_limit_bytes=58 * 1024 * 1024),
    )(*out)
    new_base, new_momentum, keys, grad_weight, grad_gain = out
    return new_base.reshape(-1), new_momentum.reshape(-1), keys[None], grad_weight[None], grad_gain


def solution(mesh):
    placed = (
        P("rep", "fsdp"),
        P("rep", "fsdp"),
        P("fsdp"),
        P("fsdp"),
        P("rep", "fsdp", None),
        P("rep", "fsdp"),
        P("rep", "fsdp", None),
    )
    return jax.shard_map(
        shards,
        mesh=mesh,
        in_specs=placed,
        out_specs=(
            P("fsdp"),
            P("fsdp"),
            P("rep", "fsdp", None),
            P("rep", "fsdp", None),
            P("rep", "fsdp"),
        ),
        check_vma=False,
    )
```
